256 devices in a mesh: gx: 32 (over y_hi, z, core), gy: 8 (over x, y_lo).
Axes of the slice: x: 4, y: 4 (y_hi: 2, y_lo: 2; y = y_hi * 2 + y_lo), z: 8, core: 2. Of those that a mesh axis runs over, the one named last changes fastest.
Arguments:
- state: float32 [6, 2048, 4096], P(None, 'gx', 'gy'), may hold values from -1 to 1
- grade: int32 [2048, 4096], P('gx', 'gy'), may hold values from 0 to 15
- table: float32 [6, 16], replicated, may hold values from 0.02 to 1.5, as said below
Outputs:
- final_state: float32 [6, 2048, 4096], P(None, 'gx', 'gy')
The draws below stay inside these ranges and needn't reach their ends.
Inputs may be any that keep to these rules, and one draw needn't show every extreme that they name: `table`: every entry is positive; row rate lies in 0.02 to 0.5, the others in 0.2 to 1.5.
All inputs are finite; a program needn't handle non-finite values.
Results may differ from the reference program's by a relative error of at most 0.0003.
Values sent between devices are 32-bit elements; how exact they have to be, the bound alone decides.
No kernel may reach another device: no remote copies, remote signals or barrier semaphores. Data moves between devices by JAX's collectives and lax.ppermute only.
A program may use at most 64 MiB of HBM per device.

```python
import jax
import jax.numpy as jnp
from jax import lax

STEPS = 8
SWEEPS = 3
FIELDS = 6
PARAMS = 6
GRADES = 16
NX = 2048
NY = 4096


def draw_table(key, part):
    key = jax.random.fold_in(key, 7)
    base = jax.random.uniform(key, (PARAMS, GRADES), jnp.float32)
    lows = jnp.array([0.5, 0.3, 0.2, 0.5, 0.02, 0.2], jnp.float32)[:, None]
    highs = jnp.array([1.5, 1.0, 0.5, 1.0, 0.5, 1.0], jnp.float32)[:, None]
    linear = lows + (highs - lows) * base
    logs = jnp.exp(jnp.log(lows) + (jnp.log(highs) - jnp.log(lows)) * base)
    is_rate = (jnp.arange(PARAMS) == 4)[:, None]
    return jnp.where(is_rate, logs, linear).astype(jnp.float32)


def plant(entries, stream_key, low, largest):
    longest = entries.shape.index(max(entries.shape))
    spots = []
    for shift in (0, 1):
        where = [jax.random.randint(jax.random.fold_in(stream_key, axis), (), 0, length) for axis, length in enumerate(entries.shape)]
        where[longest] = (where[longest] + shift) % entries.shape[longest]
        spots.append(tuple(where))
    return entries.at[spots[0]].set(low).at[spots[1]].set(largest)


def block_levels(own_key, shape, split, smallest, largest):
    loudness = 1.0
    for dim, parts in split:
        heights = jax.random.uniform(jax.random.fold_in(jax.random.fold_in(own_key, 6), dim), (parts,), jnp.float32, smallest / len(split), largest / len(split))
        loudness = loudness * jnp.repeat(jnp.exp(heights), shape[dim] // parts).reshape((-1,) + (1,) * (len(shape) - 1 - dim))
    return loudness


def gaussian(rng, extent, deviation, reach, cuts=(), kind=jnp.bfloat16):
    values = jax.random.normal(rng, extent, jnp.float32) * deviation
    if len(cuts) > 0:
        values = block_levels(rng, extent, cuts, -0.22, 0.18) * values
    return jnp.clip(values, min=-reach, max=reach).astype(kind)


def setup_inputs(seed: int = 0) -> dict:
    seeds = jax.random.split(jax.random.key(seed), 4)
    state = gaussian(seeds[0], (FIELDS, NX, NY), 0.2, 1.0, ((1, 32), (2, 8)), jnp.float32)
    grade = plant(jax.random.randint(seeds[1], (NX, NY), 0, GRADES), jax.random.fold_in(seeds[1], 1), 0, GRADES - 1).astype(jnp.int32)
    table = draw_table(jax.random.fold_in(seeds[3], 71), 0)
    return dict(state=state, grade=grade, table=table)


DT = 0.2


def corner_mean(values):
    return 0.25 * (values[:-1, :-1] + values[1:, :-1] + values[:-1, 1:] + values[1:, 1:])


def advance(fields, params, ycol, ny):
    ux, uy, vx, vy, wx, wy = fields[0], fields[1], fields[2], fields[3], fields[4], fields[5]
    lam, shear, beta, rinv, rate, eta = params[0], params[1], params[2], params[3], params[4], params[5]
    live = ((ycol >= 0) & (ycol < ny)).astype(jnp.float32)
    keep = live[:-1][None, :]
    exx = ux[1:, :-1] - ux[:-1, :-1]
    eyy = uy[:-1, 1:] - uy[:-1, :-1]
    exy = 0.5 * ((ux[:-1, 1:] - ux[:-1, :-1]) + (uy[1:, :-1] - uy[:-1, :-1]))
    lam_s = corner_mean(lam)
    mu_s = corner_mean(shear)
    beta_s = corner_mean(beta)
    trace = exx + eyy
    sxx = (lam_s * trace + 2.0 * mu_s * exx + beta_s * exx * exx * exx) * keep
    syy = (lam_s * trace + 2.0 * mu_s * eyy + beta_s * eyy * eyy * eyy) * keep
    sxy = (2.0 * mu_s * exy + beta_s * exy * exy * exy) * keep
    force_x = (sxx[1:, 1:] - sxx[:-1, 1:]) + (sxy[1:, 1:] - sxy[1:, :-1])
    force_y = (sxy[1:, 1:] - sxy[:-1, 1:]) + (syy[1:, 1:] - syy[1:, :-1])
    keep_c = live[1:-1][None, :]
    rinv_c = rinv[1:-1, 1:-1]
    rate_c = rate[1:-1, 1:-1]
    eta_c = eta[1:-1, 1:-1]
    wx_c = wx[1:-1, 1:-1]
    wy_c = wy[1:-1, 1:-1]
    new_vx = (vx[1:-1, 1:-1] + DT * rinv_c * (force_x - wx_c)) * keep_c
    new_vy = (vy[1:-1, 1:-1] + DT * rinv_c * (force_y - wy_c)) * keep_c
    new_wx = (wx_c + rate_c * (eta_c * force_x - wx_c)) * keep_c
    new_wy = (wy_c + rate_c * (eta_c * force_y - wy_c)) * keep_c
    new_ux = (ux[1:-1, 1:-1] + DT * new_vx) * keep_c
    new_uy = (uy[1:-1, 1:-1] + DT * new_vy) * keep_c
    return jnp.stack([new_ux, new_uy, new_vx, new_vy, new_wx, new_wy])


def reference(state, grade, table):
    ycol = jnp.arange(-1, NY + 1, dtype=jnp.int32)
    grade_pad = jnp.pad(grade, ((1, 1), (1, 1)), mode="wrap")
    params = table[:, grade_pad]

    def one_step(index, current):
        padded = jnp.pad(current, ((0, 0), (1, 1), (0, 0)), mode="wrap")
        padded = jnp.pad(padded, ((0, 0), (0, 0), (1, 1)))
        return advance(padded, params, ycol, NY)

    return lax.fori_loop(0, SWEEPS * STEPS, one_step, state)
```

```python
import functools

import jax
import jax.numpy as jnp
from jax import lax
from jax.experimental import pallas as pl
from jax.experimental.pallas import tpu as pltpu
from jax.sharding import PartitionSpec as P

STEPS = 24
DT = 0.2
F32 = jnp.float32
H = 24
CT = 5
EDGE = 4
PACK = 4

VMEM = pl.BlockSpec(memory_space=pltpu.VMEM)
SMEM = pl.BlockSpec(memory_space=pltpu.SMEM)


def lanes():
    return lax.broadcasted_iota(jnp.int32, (8, 128), 1)


def sublanes():
    return lax.broadcasted_iota(jnp.int32, (8, 128), 0)


def edge_live(gy, count, width):
    right = jnp.where(gy < count - 1, 1, 0)
    left = jnp.where(gy > 0, 1, 0)
    return jnp.where(lanes() < 64, right, left) > 0


def pack_y_kernel(state_ref, grade_ref, left_ref, right_ref):
    rows = state_ref.shape[1]
    group = rows // PACK
    lane = lanes()

    def read(field, row, col):
        if field < 6:
            return state_ref[field, row : row + 8, col : col + 128]
        return grade_ref[row : row + 8, col : col + 128].astype(F32)

    last = state_ref.shape[2] - 128
    for field in range(7):
        for k in range(group // 8):
            to_left = None
            to_right = None
            for q in range(PACK):
                row = q * group + 8 * k
                a = read(field, row, 0)
                b = read(field, row, last)
                if q:
                    a = pltpu.roll(a, 32 * q, 1)
                b = pltpu.roll(b, 32 * q + H, 1)
                here = lane >= 32 * q
                to_left = a if q == 0 else jnp.where(here, a, to_left)
                to_right = b if q == 0 else jnp.where(here, b, to_right)
            left_ref[field, 8 * k : 8 * k + 8, :] = to_left
            right_ref[field, 8 * k : 8 * k + 8, :] = to_right


def pack_x_kernel(count, gy_ref, state_ref, grade_ref, from_left_ref, from_right_ref, edge_ref, up_ref, down_ref):
    rows = state_ref.shape[1]
    group = rows // PACK
    lane = lanes()
    live = edge_live(gy_ref[0], count, state_ref.shape[2])
    for field in range(7):
        for k in range(group // 8):
            right = from_right_ref[field, 8 * k : 8 * k + 8, :]
            left = from_left_ref[field, 8 * k : 8 * k + 8, :]
            for q in range(PACK):
                r = right if q == 0 else pltpu.roll(right, 128 - 32 * q, 1)
                s = pltpu.roll(left, (128 - H - 32 * q) % 128, 1)
                both = jnp.where(lane < H, r, jnp.where(lane >= 128 - H, s, 0.0))
                if field < 6:
                    both = jnp.where(live, both, 0.0)
                row = q * group + 8 * k
                edge_ref[field, row : row + 8, :] = both
                if row < H:
                    up_ref[field, EDGE, row : row + 8, :] = both
                if row >= rows - H:
                    down_ref[field, EDGE, row - rows + H : row - rows + H + 8, :] = both
    for field in range(7):
        for c in range(CT - 1):
            cols = slice(128 * c, 128 * c + 128)
            if field < 6:
                up_ref[field, c] = state_ref[field, 0:H, cols]
                down_ref[field, c] = state_ref[field, rows - H : rows, cols]
            else:
                up_ref[field, c] = grade_ref[0:H, cols].astype(F32)
                down_ref[field, c] = grade_ref[rows - H : rows, cols].astype(F32)


def tables(table_ref, tab):
    tab[0:6, 0:16] = table_ref[...]

    def row(q):
        return jnp.broadcast_to(tab[q : q + 1, :], (8, 128))

    rate = row(4)
    return (
        0.25 * row(0),
        0.25 * row(1),
        0.25 * row(2),
        (DT * DT) * row(3),
        1.0 - rate,
        rate * row(5),
    )


def look_up(tabs, grade):
    return [jnp.take_along_axis(t, grade, axis=1) for t in tabs]


def put_raw(pr, tabs, live, grade_of, tiles, first_row):
    for k in range(tiles):
        for c in range(CT):
            lam, mu, beta, dr, om, re = look_up(tabs, grade_of(c, k))
            if c == EDGE:
                dr = jnp.where(live, dr, 0.0)
                re = jnp.where(live, re, 0.0)
            where = (c, pl.ds(first_row + 8 * k, 8), slice(None))
            pr[(0,) + where] = lam
            pr[(1,) + where] = mu
            pr[(3,) + where] = beta
            pr[(5,) + where] = dr
            pr[(6,) + where] = om
            pr[(7,) + where] = re


def put_means(pr, live, tiles):
    last = lanes() == 127
    for k in range(tiles):
        for q in (0, 1, 3):
            sums = [pr[q, c, pl.ds(8 * k, 8), :] + pr[q, c, pl.ds(8 * k + 1, 8), :] for c in range(CT)]
            moved = following(sums, last)
            for c in range(CT):
                mean = sums[c] + moved[c]
                if c == EDGE:
                    mean = jnp.where(live, mean, 0.0)
                where = (c, pl.ds(8 * k, 8), slice(None))
                if q == 0:
                    pr[(0,) + where] = mean
                elif q == 1:
                    pr[(1,) + where] = 2.0 * mean
                    pr[(2,) + where] = mean
                else:
                    pr[(3,) + where] = mean
                    pr[(4,) + where] = 0.125 * mean


def following(tiles, last):
    rolled = [pltpu.roll(x, 127, 1) for x in tiles]
    return [jnp.where(last, rolled[(c + 1) % CT], rolled[c]) for c in range(CT)]


def preceding(tiles, first):
    rolled = [pltpu.roll(x, 1, 1) for x in tiles]
    return [jnp.where(first, rolled[(c - 1) % CT], rolled[c]) for c in range(CT)]


def read(ref, plane, rows):
    return [ref[plane, c, rows, :] for c in range(CT)]


def stresses(pr, rows, ux, uy, uxn, uyn):
    lane = lanes()
    last = lane == 127
    first = lane == 0
    uxr = following(ux, last)
    uyr = following(uy, last)
    lam, mu2, mu, beta, beta8 = [read(pr, q, rows) for q in range(5)]
    sxx, sxy, syy = [], [], []
    for c in range(CT):
        exx = uxn[c] - ux[c]
        eyy = uyr[c] - uy[c]
        g = (uxr[c] - ux[c]) + (uyn[c] - uy[c])
        trace = lam[c] * (exx + eyy)
        sxx.append(trace + exx * (mu2[c] + beta[c] * (exx * exx)))
        syy.append(trace + eyy * (mu2[c] + beta[c] * (eyy * eyy)))
        sxy.append(g * (mu[c] + beta8[c] * (g * g)))
    sxy_l = preceding(sxy, first)
    syy_l = preceding(syy, first)
    gx = [sxx[c] + (sxy[c] - sxy_l[c]) for c in range(CT)]
    gy = [sxy[c] + (syy[c] - syy_l[c]) for c in range(CT)]
    return gx, gy, sxx, sxy


def update(st, pr, rows, ux, uy, gx, gy, px, py):
    dr, om, re = [read(pr, q, rows) for q in (5, 6, 7)]
    vx, vy, wx, wy = [read(st, q, rows) for q in (2, 3, 4, 5)]
    for c in range(CT):
        fx = gx[c] - px[c]
        fy = gy[c] - py[c]
        new_vx = vx[c] + dr[c] * (fx - wx[c])
        new_vy = vy[c] + dr[c] * (fy - wy[c])
        st[2, c, rows, :] = new_vx
        st[3, c, rows, :] = new_vy
        st[4, c, rows, :] = om[c] * wx[c] + re[c] * fx
        st[5, c, rows, :] = om[c] * wy[c] + re[c] * fy
        st[0, c, rows, :] = ux[c] + new_vx
        st[1, c, rows, :] = uy[c] + new_vy


def interior_kernel(count, gy_ref, table_ref, state_ref, grade_ref, edge_ref, keep_ref, tail_ref, trace_ref, st, pr, ss, tab):
    rows = state_ref.shape[1]
    live = edge_live(gy_ref[0], count, state_ref.shape[2])
    tabs = tables(table_ref, tab)

    def grade_of(c, k):
        if c == EDGE:
            return edge_ref[6, 8 * k : 8 * k + 8, :].astype(jnp.int32)
        return grade_ref[8 * k : 8 * k + 8, 128 * c : 128 * c + 128]

    put_raw(pr, tabs, live, grade_of, rows // 8, 0)
    put_means(pr, live, rows // 8)
    for f in range(6):
        for c in range(CT):
            block = edge_ref[f] if c == EDGE else state_ref[f, :, 128 * c : 128 * c + 128]
            if f in (2, 3):
                block = DT * block
            st[f, c, 0:rows, :] = block
            tail_ref[f, c, H - 1 : H, :] = block[rows - 1 : rows]

    for g in range(STEPS // 4):
        n = rows // 8 - g

        def body(k, carry, n=n, g=g):
            base = 4 * g + k

            def at(offset):
                return pl.ds(base + offset, 8, stride=n)

            ux, uy = read(st, 0, at(0)), read(st, 1, at(0))
            uxn, uyn = read(st, 0, at(1)), read(st, 1, at(1))
            gx0, gy0, px, py = stresses(pr, at(0), ux, uy, uxn, uyn)
            for c in range(CT):
                trace_ref[0, c, pl.ds(base, 1), :] = gx0[c][0:1]
                trace_ref[1, c, pl.ds(base, 1), :] = gy0[c][0:1]
            for r in range(n):
                ux, uy = uxn, uyn
                for c in range(CT):
                    ss[0, c, at(r), :] = px[c]
                    ss[1, c, at(r), :] = py[c]
                if r < n - 1:
                    uxn, uyn = read(st, 0, at(r + 2)), read(st, 1, at(r + 2))
                    gx, gy, qx, qy = stresses(pr, at(r + 1), ux, uy, uxn, uyn)
                else:
                    gx = [pltpu.roll(v, 7, 0) for v in gx0]
                    gy = [pltpu.roll(v, 7, 0) for v in gy0]
                    qx, qy = px, py
                update(st, pr, at(r + 1), ux, uy, gx, gy, px, py)
                px, py = qx, qy
            row = rows - 2 - base
            for c in range(CT):
                for q in range(2):
                    trace_ref[2 + q, c, pl.ds(base, 1), :] = ss[q, c, pl.ds(row, 1), :]

                @pl.when(base < STEPS - 1)
                def _():
                    for f in range(6):
                        tail_ref[f, c, pl.ds(H - 2 - base, 1), :] = st[f, c, pl.ds(row, 1), :]

            return carry

        lax.fori_loop(0, 4, body, 0)
    for f in range(6):
        for c in range(CT):
            keep_ref[f, c] = st[f, c, 0 : rows - H, :]


def exterior_kernel(
    count, gy_ref, table_ref, grade_ref, edge_ref, keep_ref, tail_ref, trace_ref, top_ref, bottom_ref, out_ref, sa, pa, sb, pb, tab
):
    rows = grade_ref.shape[0]
    live = edge_live(gy_ref[0], count, grade_ref.shape[1])
    tabs = tables(table_ref, tab)
    near = H // 8

    def grades(first, halo_ref):
        def grade_of(c, k):
            if halo_ref is not None:
                return halo_ref[6, c, 8 * k : 8 * k + 8, :].astype(jnp.int32)
            row = first + 8 * k
            if c == EDGE:
                return edge_ref[6, row : row + 8, :].astype(jnp.int32)
            return grade_ref[row : row + 8, 128 * c : 128 * c + 128]

        return grade_of

    put_raw(pa, tabs, live, grades(0, top_ref), near, 0)
    put_raw(pa, tabs, live, grades(0, None), near, H)
    put_raw(pb, tabs, live, grades(rows - H, None), near, 0)
    put_raw(pb, tabs, live, grades(0, bottom_ref), near, H)
    put_means(pa, live, 2 * near)
    put_means(pb, live, 2 * near)
    for f in range(6):
        for c in range(CT):
            top = top_ref[f, c]
            bottom = bottom_ref[f, c]
            if f in (2, 3):
                top = DT * top
                bottom = DT * bottom
            sa[f, c, 0:H, :] = top
            sa[f, c, H : 2 * H, :] = keep_ref[f, c, 0:H, :]
            sb[f, c, 0:H, :] = tail_ref[f, c]
            sb[f, c, H : 2 * H, :] = bottom

    sub = sublanes()
    n = near

    def body(base, carry):
        def at(offset):
            return pl.ds(base + offset, 8, stride=n)

        def bt(offset):
            return pl.ds(H - 1 - base + offset, 8, stride=n)

        def trace(q):
            return [jnp.broadcast_to(trace_ref[q, c, pl.ds(base, 1), :], (8, 128)) for c in range(CT)]

        ux, uy = read(sa, 0, at(0)), read(sa, 1, at(0))
        uxn, uyn = read(sa, 0, at(1)), read(sa, 1, at(1))
        gx0, gy0, px, py = stresses(pa, at(0), ux, uy, uxn, uyn)
        for r in range(n):
            ux, uy = uxn, uyn
            if r < n - 1:
                uxn, uyn = read(sa, 0, at(r + 2)), read(sa, 1, at(r + 2))
                gx, gy, qx, qy = stresses(pa, at(r + 1), ux, uy, uxn, uyn)
            else:
                tx, ty = trace(0), trace(1)
                gx = [jnp.where(sub == 7, tx[c], pltpu.roll(gx0[c], 7, 0)) for c in range(CT)]
                gy = [jnp.where(sub == 7, ty[c], pltpu.roll(gy0[c], 7, 0)) for c in range(CT)]
                qx, qy = px, py
            update(sa, pa, at(r + 1), ux, uy, gx, gy, px, py)
            px, py = qx, qy
        uxs = [read(sb, 0, bt(r)) for r in range(n + 1)]
        uys = [read(sb, 1, bt(r)) for r in range(n + 1)]
        tx, ty = trace(2), trace(3)
        gz, hz, px, py = stresses(pb, bt(n - 1), uxs[n - 1], uys[n - 1], uxs[n], uys[n])
        px = [jnp.where(sub == 0, tx[c], pltpu.roll(px[c], 1, 0)) for c in range(CT)]
        py = [jnp.where(sub == 0, ty[c], pltpu.roll(py[c], 1, 0)) for c in range(CT)]
        for r in range(n):
            if r < n - 1:
                gx, gy, qx, qy = stresses(pb, bt(r), uxs[r], uys[r], uxs[r + 1], uys[r + 1])
            else:
                gx, gy, qx, qy = gz, hz, None, None
            update(sb, pb, bt(r), uxs[r], uys[r], gx, gy, px, py)
            px, py = qx, qy
        return carry

    lax.fori_loop(0, STEPS, body, 0)
    for f in range(6):
        for c in range(CT - 1):
            cols = slice(128 * c, 128 * c + 128)
            scale = 1.0 / DT if f in (2, 3) else None
            for first, block in ((0, sa[f, c, H : 2 * H, :]), (H, keep_ref[f, c, H:, :]), (rows - H, sb[f, c, 0:H, :])):
                out_ref[f, first : first + block.shape[0], cols] = block if scale is None else scale * block


def params(bytes_, flops):
    return dict(
        compiler_params=pltpu.CompilerParams(vmem_limit_bytes=24 * 2**20),
        cost_estimate=pl.CostEstimate(flops=flops, bytes_accessed=bytes_, transcendentals=0),
    )


def ring(count, step):
    return [(i, (i + step) % count) for i in range(count)]


def shards(state, grade, table):
    fields, rows, cols = state.shape
    nx = lax.axis_size("gx")
    ny = lax.axis_size("gy")
    gy = jnp.full((1,), lax.axis_index("gy"), jnp.int32)
    packed = jax.ShapeDtypeStruct((7, rows // PACK, 128), F32)
    to_left, to_right = pl.pallas_call(
        pack_y_kernel,
        out_shape=(packed, packed),
        in_specs=[VMEM, VMEM],
        out_specs=(VMEM, VMEM),
        **params(10**6, 10**5),
    )(state, grade)
    from_left = lax.ppermute(to_right, "gy", ring(ny, 1))
    from_right = lax.ppermute(to_left, "gy", ring(ny, -1))
    strip = jax.ShapeDtypeStruct((7, CT, H, 128), F32)
    edge, to_up, to_down = pl.pallas_call(
        functools.partial(pack_x_kernel, ny),
        out_shape=(jax.ShapeDtypeStruct((7, rows, 128), F32), strip, strip),
        in_specs=[SMEM] + [VMEM] * 4,
        out_specs=(VMEM,) * 3,
        **params(2 * 10**6, 10**5),
    )(gy, state, grade, from_left, from_right)
    top = lax.ppermute(to_down, "gx", ring(nx, 1))
    bottom = lax.ppermute(to_up, "gx", ring(nx, -1))
    keep, tail, trace = pl.pallas_call(
        functools.partial(interior_kernel, ny),
        out_shape=(
            jax.ShapeDtypeStruct((6, CT, rows - H, 128), F32),
            jax.ShapeDtypeStruct((6, CT, H, 128), F32),
            jax.ShapeDtypeStruct((4, CT, H, 128), F32),
        ),
        in_specs=[SMEM] + [VMEM] * 4,
        out_specs=(VMEM,) * 3,
        scratch_shapes=[
            pltpu.VMEM((6, CT, rows + 8, 128), F32),
            pltpu.VMEM((8, CT, rows + 8, 128), F32),
            pltpu.VMEM((2, CT, rows + 8, 128), F32),
            pltpu.VMEM((8, 128), F32),
        ],
        **params(4 * 10**6, 10**9),
    )(gy, table, state, grade, edge)
    return pl.pallas_call(
        functools.partial(exterior_kernel, ny),
        out_shape=jax.ShapeDtypeStruct((fields, rows, cols), F32),
        in_specs=[SMEM] + [VMEM] * 8,
        out_specs=VMEM,
        scratch_shapes=[
            pltpu.VMEM((6, CT, 2 * H + 8, 128), F32),
            pltpu.VMEM((8, CT, 2 * H + 8, 128), F32),
            pltpu.VMEM((6, CT, 2 * H + 8, 128), F32),
            pltpu.VMEM((8, CT, 2 * H + 8, 128), F32),
            pltpu.VMEM((8, 128), F32),
        ],
        **params(4 * 10**6, 10**9),
    )(gy, table, grade, edge, keep, tail, trace, top, bottom)


def solution(mesh):
    placed = (P(None, "gx", "gy"), P("gx", "gy"), P())
    return jax.shard_map(
        shards, mesh=mesh, in_specs=placed, out_specs=P(None, "gx", "gy"), check_vma=False
    )
```

```python
import functools

import jax
import jax.numpy as jnp
from jax import lax
from jax.experimental import pallas as pl
from jax.experimental.pallas import tpu as pltpu
from jax.sharding import PartitionSpec as P

STEPS = 24
DT = 0.2
F32 = jnp.float32
H = 24
CT = 5
EDGE = 4
MAIN = (0, 1, 2, 3)
ALL = (0, 1, 2, 3, 4)
SWAP = 8
MID = 20
PACK = 4

VMEM = pl.BlockSpec(memory_space=pltpu.VMEM)
SMEM = pl.BlockSpec(memory_space=pltpu.SMEM)
ANY = pl.BlockSpec(memory_space=pl.ANY)
HBM = pl.BlockSpec(memory_space=pltpu.HBM)


def lanes():
    return lax.broadcasted_iota(jnp.int32, (8, 128), 1)


def sublanes():
    return lax.broadcasted_iota(jnp.int32, (8, 128), 0)


def edge_live(gy, count):
    right = jnp.where(gy < count - 1, 1, 0)
    left = jnp.where(gy > 0, 1, 0)
    lane = lanes()
    return jnp.where(lane < H, left, jnp.where(lane >= 128 - H, right, 1)) > 0


def pack_y_kernel(state_hbm, grade_hbm, left_ref, right_ref, grade_ref, ends, sems):
    rows, cols = state_hbm.shape[1:]
    group = rows // PACK
    lane = lanes()
    copies = []
    for f in range(6):
        for side, first in enumerate((0, cols - 128)):
            source = state_hbm.at[f, :, pl.ds(first, 128)]
            copies.append(pltpu.make_async_copy(source, ends.at[f, side], sems.at[2 * f + side]))
    copies.append(pltpu.make_async_copy(grade_hbm, grade_ref, sems.at[12]))
    for copy in copies:
        copy.start()

    def read(field, row, side):
        if field < 6:
            return ends[field, side, row : row + 8, :]
        first = side * (cols - 128)
        return grade_ref[row : row + 8, first : first + 128].astype(F32)

    for field in range(7):
        for copy in copies[2 * field : 2 * field + 2]:
            copy.wait()
        for k in range(group // 8):
            to_left = None
            to_right = None
            for q in range(PACK):
                row = q * group + 8 * k
                a = read(field, row, 0)
                b = read(field, row, 1)
                if q:
                    a = pltpu.roll(a, 32 * q, 1)
                b = pltpu.roll(b, 32 * q + H, 1)
                here = lane >= 32 * q
                to_left = a if q == 0 else jnp.where(here, a, to_left)
                to_right = b if q == 0 else jnp.where(here, b, to_right)
            left_ref[field, 8 * k : 8 * k + 8, :] = to_left
            right_ref[field, 8 * k : 8 * k + 8, :] = to_right


def pack_x_kernel(count, gy_ref, state_ref, grade_ref, from_left_ref, from_right_ref, _, edge_ref, up_ref, down_ref):
    rows, cols = state_ref.shape[1:]
    group = rows // PACK
    lane = lanes()
    live = edge_live(gy_ref[0], count)
    for field in range(7):
        for k in range(group // 8):
            right = from_right_ref[field, 8 * k : 8 * k + 8, :]
            left = from_left_ref[field, 8 * k : 8 * k + 8, :]
            for q in range(PACK):
                r = pltpu.roll(right, (128 - H - 32 * q) % 128, 1)
                s = left if q == 0 else pltpu.roll(left, 128 - 32 * q, 1)
                halo = jnp.where(lane < 64, s, r)
                if field < 6:
                    halo = jnp.where(live, halo, 0.0)
                row = q * group + 8 * k
                if field < 6:
                    first = state_ref[field, row : row + 8, 0:128]
                    last = state_ref[field, row : row + 8, cols - 128 : cols]
                else:
                    first = grade_ref[row : row + 8, 0:128].astype(F32)
                    last = grade_ref[row : row + 8, cols - 128 : cols].astype(F32)
                own = jnp.where(lane < 64, pltpu.roll(first, H, 1), pltpu.roll(last, 128 - H, 1))
                both = jnp.where((lane < H) | (lane >= 128 - H), halo, own)
                edge_ref[field, row : row + 8, :] = both
                if row < H:
                    up_ref[field, EDGE, row : row + 8, :] = both
                if row >= rows - H:
                    down_ref[field, EDGE, row - rows + H : row - rows + H + 8, :] = both
    for field in range(7):
        for c in MAIN:
            part = slice(128 * c, 128 * c + 128)
            if field < 6:
                up_ref[field, c] = state_ref[field, 0:H, part]
                down_ref[field, c] = state_ref[field, rows - H : rows, part]
            else:
                up_ref[field, c] = grade_ref[0:H, part].astype(F32)
                down_ref[field, c] = grade_ref[rows - H : rows, part].astype(F32)


def tables(table_ref, tab):
    tab[0:6, 0:16] = table_ref[...]

    def row(q):
        return jnp.broadcast_to(tab[q : q + 1, :], (8, 128))

    rate = row(4)
    return (
        0.25 * row(0),
        0.25 * row(1),
        0.25 * row(2),
        (DT * DT) * row(3),
        1.0 - rate,
        rate * row(5),
    )


def put_raw(pr, tabs, live, grade_of, cols, tiles, first_row, planes_=(0, 1, 3, 5, 6, 7)):
    for k in range(tiles):
        for c in cols:
            grade = grade_of(c, k)
            for t, q in enumerate((0, 1, 3, 5, 6, 7)):
                if q not in planes_:
                    continue
                value = jnp.take_along_axis(tabs[t], grade, axis=1)
                if c == EDGE and q in (5, 7):
                    value = jnp.where(live, value, 0.0)
                pr[q][c][pl.ds(first_row + 8 * k, 8), :] = value


def put_means(pr, live, cols, first_tile, tiles):
    for k in range(first_tile, first_tile + tiles):
        here = pl.ds(8 * k, 8)
        for q in (0, 1, 3):
            sums = {c: pr[q][c][here, :] + pr[q][c][pl.ds(8 * k + 1, 8), :] for c in cols}
            moved = following(sums)
            for c in cols:
                mean = sums[c] + moved[c]
                if c == EDGE:
                    mean = jnp.where(live, mean, 0.0)
                if q == 0:
                    pr[0][c][here, :] = mean
                elif q == 1:
                    pr[1][c][here, :] = 2.0 * mean
                    pr[2][c][here, :] = mean
                else:
                    pr[3][c][here, :] = mean
                    pr[4][c][here, :] = 0.125 * mean


def following(tiles):
    last = lanes() == 127
    rolled = {c: pltpu.roll(x, 127, 1) for c, x in tiles.items()}
    return {c: jnp.where(last, rolled[c + 1], rolled[c]) if c + 1 in MAIN and c in MAIN else rolled[c] for c in tiles}


def preceding(tiles):
    first = lanes() == 0
    rolled = {c: pltpu.roll(x, 1, 1) for c, x in tiles.items()}
    return {c: jnp.where(first, rolled[c - 1], rolled[c]) if c - 1 in MAIN and c in MAIN else rolled[c] for c in tiles}


def read(refs, rows):
    return {c: ref[rows, :] for c, ref in refs.items()}


def stresses(pr, rows, ux, uy, uxn, uyn):
    uxr = following(ux)
    uyr = following(uy)
    lam, mu2, mu, beta, beta8 = [read({c: pr[q][c] for c in ux}, rows) for q in range(5)]
    sxx, sxy, syy = {}, {}, {}
    for c in ux:
        exx = uxn[c] - ux[c]
        eyy = uyr[c] - uy[c]
        g = (uxr[c] - ux[c]) + (uyn[c] - uy[c])
        trace = lam[c] * (exx + eyy)
        sxx[c] = trace + exx * (mu2[c] + beta[c] * (exx * exx))
        syy[c] = trace + eyy * (mu2[c] + beta[c] * (eyy * eyy))
        sxy[c] = g * (mu[c] + beta8[c] * (g * g))
    sxy_l = preceding(sxy)
    syy_l = preceding(syy)
    gx = {c: sxx[c] + (sxy[c] - sxy_l[c]) for c in ux}
    gy = {c: sxy[c] + (syy[c] - syy_l[c]) for c in ux}
    return gx, gy, sxx, sxy


def update(st, pr, rows, ux, uy, gx, gy, px, py):
    dr, om, re = [read({c: pr[q][c] for c in ux}, rows) for q in (5, 6, 7)]
    vx, vy, wx, wy = [read({c: st[q][c] for c in ux}, rows) for q in (2, 3, 4, 5)]
    for c in ux:
        fx = gx[c] - px[c]
        fy = gy[c] - py[c]
        new_vx = vx[c] + dr[c] * (fx - wx[c])
        new_vy = vy[c] + dr[c] * (fy - wy[c])
        st[2][c][rows, :] = new_vx
        st[3][c][rows, :] = new_vy
        st[4][c][rows, :] = om[c] * wx[c] + re[c] * fx
        st[5][c][rows, :] = om[c] * wy[c] + re[c] * fy
        st[0][c][rows, :] = ux[c] + new_vx
        st[1][c][rows, :] = uy[c] + new_vy


def tiles_of(ref, cols):
    return [{c: ref.at[q, c] for c in cols} for q in range(ref.shape[0])]


def swap(st, first_row, rows):
    lane = lanes()
    inner = (lane >= H + MID) & (lane < 128 - H - MID)
    tiles = [pl.ds(8 * k, 8) for k in range(first_row // 8, (first_row + rows) // 8)]
    for f in range(6):
        old = [(st[f][EDGE][here, :], st[f][0][here, :], st[f][MAIN[-1]][here, :]) for here in tiles]
        new = []
        for edge, first, last in old:
            own = jnp.where(lane < 64, pltpu.roll(first, H, 1), pltpu.roll(last, 128 - H, 1))
            new.append((
                jnp.where(inner, own, edge),
                jnp.where(lane < MID, pltpu.roll(edge, 128 - H, 1), first),
                jnp.where(lane >= 128 - MID, pltpu.roll(edge, H, 1), last),
            ))
        for here, (edge, first, last) in zip(tiles, new):
            st[f][EDGE][here, :] = edge
            st[f][0][here, :] = first
            st[f][MAIN[-1]][here, :] = last


def trapezoid(st, pr, ss, cols, rows, groups, trace_ref, tail_ref):
    for g in groups:
        n = rows // 8 - g
        n = n + 1 if n == 8 else n

        def body(k, carry, n=n, g=g):
            base = 4 * g + k

            def at(offset):
                return pl.ds(base + offset, 8, stride=n)

            def u(f, offset):
                return read({c: st[f][c] for c in cols}, at(offset))

            ux, uy, uxn, uyn = u(0, 0), u(1, 0), u(0, 1), u(1, 1)
            gx0, gy0, px, py = stresses(pr, at(0), ux, uy, uxn, uyn)
            for c in cols:
                trace_ref[0, c, pl.ds(base, 1), :] = gx0[c][0:1]
                trace_ref[1, c, pl.ds(base, 1), :] = gy0[c][0:1]
            for r in range(n):
                ux, uy = uxn, uyn
                for c in cols:
                    ss[0, c, at(r), :] = px[c]
                    ss[1, c, at(r), :] = py[c]
                if r < n - 1:
                    uxn, uyn = u(0, r + 2), u(1, r + 2)
                    gx, gy, qx, qy = stresses(pr, at(r + 1), ux, uy, uxn, uyn)
                else:
                    gx = {c: pltpu.roll(v, 7, 0) for c, v in gx0.items()}
                    gy = {c: pltpu.roll(v, 7, 0) for c, v in gy0.items()}
                    qx, qy = px, py
                update(st, pr, at(r + 1), ux, uy, gx, gy, px, py)
                px, py = qx, qy
            row = pl.ds(rows - 2 - base, 1)
            for c in cols:
                for q in range(2):
                    trace_ref[2 + q, c, pl.ds(base, 1), :] = ss[q, c, row, :]
                for f in range(6):
                    tail_ref[f, c, pl.ds(H - 1 - base, 1), :] = st[f][c][row, :]
            return carry

        lax.fori_loop(0, 4, body, 0)


def own_kernel(table_ref, state_ref, grade_ref, st_ref, pr_ref, tail_ref, trace_ref, ss, tab):
    rows = state_ref.shape[1]
    tabs = tables(table_ref, tab)
    st, pr = tiles_of(st_ref, MAIN), tiles_of(pr_ref, MAIN)

    def grade_of(c, k):
        return grade_ref[8 * k : 8 * k + 8, 128 * c : 128 * c + 128]

    put_raw(pr, tabs, None, grade_of, MAIN, rows // 8, 0)
    put_means(pr, None, MAIN, 0, rows // 8)
    for f in range(6):
        for c in MAIN:
            block = state_ref[f, :, 128 * c : 128 * c + 128]
            if f in (2, 3):
                block = DT * block
            st[f][c][0:rows, :] = block
            tail_ref[f, c, H : H + 1, :] = block[rows - 1 : rows]
    trapezoid(st, pr, ss, MAIN, rows, range(SWAP // 4), trace_ref, tail_ref)


def interior_kernel(
    count, gy_ref, table_ref, edge_ref, st_ref, pr_ref, tail_in, trace_in, keep_ref, tail_ref, trace_ref, pe_ref, mid, ss, tab
):
    rows = edge_ref.shape[1]
    live = edge_live(gy_ref[0], count)
    tabs = tables(table_ref, tab)
    st = tiles_of(mid, ALL)
    pr = tiles_of(pr_ref, MAIN)
    for q in range(8):
        pr[q][EDGE] = pe_ref.at[q]

    def grade_of(c, k):
        return edge_ref[6, 8 * k : 8 * k + 8, :].astype(jnp.int32)

    put_raw(pr, tabs, live, grade_of, (EDGE,), rows // 8, 0)
    put_means(pr, live, (EDGE,), 0, rows // 8)
    for f in range(6):
        block = DT * edge_ref[f] if f in (2, 3) else edge_ref[f]
        st[f][EDGE][0:rows, :] = block
        tail_ref[f, EDGE, H : H + 1, :] = block[rows - 1 : rows]
        for c in MAIN:
            st[f][c][0:rows, :] = st_ref[f, c, 0:rows, :]
            tail_ref[f, c] = tail_in[f, c]
    for q in range(4):
        for c in MAIN:
            trace_ref[q, c] = trace_in[q, c]
    trapezoid(st, pr, ss, (EDGE,), rows, range(SWAP // 4), trace_ref, tail_ref)
    swap(st, 0, rows)
    trapezoid(st, pr, ss, ALL, rows, range(SWAP // 4, STEPS // 4), trace_ref, tail_ref)
    for f in range(6):
        for c in ALL:
            keep_ref[f, c] = st[f][c][0 : rows - H, :]


def exterior_kernel(
    count, gy_ref, table_ref, grade_ref, edge_ref, keep_ref, tail_ref, trace_ref, pr_ref, pe_ref, top_ref, bottom_ref,
    out_ref, sa_ref, pa_ref, sb_ref, pb_ref, tab,
):
    rows = grade_ref.shape[0]
    live = edge_live(gy_ref[0], count)
    tabs = tables(table_ref, tab)
    near = H // 8
    sa, pa, sb, pb = [tiles_of(ref, ALL) for ref in (sa_ref, pa_ref, sb_ref, pb_ref)]

    def halo(ref):
        return lambda c, k: ref[6, c, 8 * k : 8 * k + 8, :].astype(jnp.int32)

    def own(row):
        def grade_of(c, k):
            if c == EDGE:
                return edge_ref[6, row : row + 8, :].astype(jnp.int32)
            return grade_ref[row : row + 8, 128 * c : 128 * c + 128]

        return grade_of

    def known(q, c, first, count_):
        return pe_ref[q, first : first + count_, :] if c == EDGE else pr_ref[q, c, first : first + count_, :]

    put_raw(pa, tabs, live, halo(top_ref), ALL, near, 0)
    put_raw(pa, tabs, live, own(0), ALL, 1, H, (0, 1, 3))
    put_means(pa, live, ALL, 0, near)
    put_raw(pb, tabs, live, own(rows - 8), ALL, 1, H - 8, (0, 1, 3))
    put_raw(pb, tabs, live, halo(bottom_ref), ALL, near, H)
    put_means(pb, live, ALL, near - 1, near + 1)
    for q in range(8):
        for c in ALL:
            pa[q][c][H : 2 * H, :] = known(q, c, 0, H)
            whole = H if q > 4 else H - 8
            pb[q][c][0:whole, :] = known(q, c, rows - H, whole)
    for f in range(6):
        for c in ALL:
            top = top_ref[f, c]
            bottom = bottom_ref[f, c]
            if f in (2, 3):
                top = DT * top
                bottom = DT * bottom
            sa[f][c][0:H, :] = top
            sa[f][c][H : 2 * H, :] = keep_ref[f, c, 0:H, :]
            sb[f][c][0:H, :] = tail_ref[f, c, 1 : H + 1, :]
            sb[f][c][H : 2 * H, :] = bottom

    sub = sublanes()
    n = near

    def body(base, carry):
        def at(offset):
            return pl.ds(base + offset, 8, stride=n)

        def bt(offset):
            return pl.ds(H - 1 - base + offset, 8, stride=n)

        def trace(q):
            return [jnp.broadcast_to(trace_ref[q, c, pl.ds(base, 1), :], (8, 128)) for c in ALL]

        ux, uy = read(sa[0], at(0)), read(sa[1], at(0))
        uxn, uyn = read(sa[0], at(1)), read(sa[1], at(1))
        gx0, gy0, px, py = stresses(pa, at(0), ux, uy, uxn, uyn)
        for r in range(n):
            ux, uy = uxn, uyn
            if r < n - 1:
                uxn, uyn = read(sa[0], at(r + 2)), read(sa[1], at(r + 2))
                gx, gy, qx, qy = stresses(pa, at(r + 1), ux, uy, uxn, uyn)
            else:
                tx, ty = trace(0), trace(1)
                gx = {c: jnp.where(sub == 7, tx[c], pltpu.roll(gx0[c], 7, 0)) for c in ALL}
                gy = {c: jnp.where(sub == 7, ty[c], pltpu.roll(gy0[c], 7, 0)) for c in ALL}
                qx, qy = px, py
            update(sa, pa, at(r + 1), ux, uy, gx, gy, px, py)
            px, py = qx, qy
        uxs = [read(sb[0], bt(r)) for r in range(n + 1)]
        uys = [read(sb[1], bt(r)) for r in range(n + 1)]
        tx, ty = trace(2), trace(3)
        gz, hz, px, py = stresses(pb, bt(n - 1), uxs[n - 1], uys[n - 1], uxs[n], uys[n])
        px = {c: jnp.where(sub == 0, tx[c], pltpu.roll(px[c], 1, 0)) for c in ALL}
        py = {c: jnp.where(sub == 0, ty[c], pltpu.roll(py[c], 1, 0)) for c in ALL}
        for r in range(n):
            if r < n - 1:
                gx, gy, qx, qy = stresses(pb, bt(r), uxs[r], uys[r], uxs[r + 1], uys[r + 1])
            else:
                gx, gy, qx, qy = gz, hz, None, None
            update(sb, pb, bt(r), uxs[r], uys[r], gx, gy, px, py)
            px, py = qx, qy
        return carry

    lax.fori_loop(0, SWAP, body, 0)
    swap(sa, SWAP, H)
    swap(sb, H - 2 * SWAP, H + SWAP)
    lax.fori_loop(SWAP, STEPS, body, 0)
    lane = lanes()
    for f in range(6):
        for k in range(rows // 8):
            row = 8 * k

            def final(c):
                if row < H:
                    return sa[f][c][H + row : H + row + 8, :]
                if row < rows - H:
                    return keep_ref[f, c, row : row + 8, :]
                return sb[f][c][row - rows + H : row - rows + H + 8, :]

            edge = final(EDGE)
            for c in MAIN:
                value = final(c)
                if c == 0:
                    value = jnp.where(lane < MID, pltpu.roll(edge, 128 - H, 1), value)
                if c == MAIN[-1]:
                    value = jnp.where(lane >= 128 - MID, pltpu.roll(edge, H, 1), value)
                if f in (2, 3):
                    value = (1.0 / DT) * value
                out_ref[f, row : row + 8, 128 * c : 128 * c + 128] = value


def params(bytes_, flops):
    return dict(
        compiler_params=pltpu.CompilerParams(vmem_limit_bytes=24 * 2**20),
        cost_estimate=pl.CostEstimate(flops=flops, bytes_accessed=bytes_, transcendentals=0),
    )


def ring(count, step):
    return [(i, (i + step) % count) for i in range(count)]


def shards(state, grade, table):
    fields, rows, cols = state.shape
    nx = lax.axis_size("gx")
    ny = lax.axis_size("gy")
    gy = jnp.full((1,), lax.axis_index("gy"), jnp.int32)
    packed = jax.ShapeDtypeStruct((7, rows // PACK, 128), F32)
    to_left, to_right, grade = pl.pallas_call(
        pack_y_kernel,
        out_shape=(packed, packed, jax.ShapeDtypeStruct(grade.shape, grade.dtype)),
        in_specs=[HBM, HBM],
        out_specs=(VMEM,) * 3,
        scratch_shapes=[pltpu.VMEM((6, 2, rows, 128), F32), pltpu.SemaphoreType.DMA((13,))],
        **params(10**6, 10**5),
    )(state, grade)
    from_left = lax.ppermute(to_right, "gy", ring(ny, 1))
    from_right = lax.ppermute(to_left, "gy", ring(ny, -1))
    wide = rows + 16
    st, pr, tail, trace = pl.pallas_call(
        own_kernel,
        out_shape=(
            jax.ShapeDtypeStruct((6, CT - 1, wide, 128), F32),
            jax.ShapeDtypeStruct((8, CT - 1, wide, 128), F32),
            jax.ShapeDtypeStruct((6, CT - 1, H + 8, 128), F32),
            jax.ShapeDtypeStruct((4, CT - 1, H, 128), F32),
        ),
        in_specs=[VMEM] * 3,
        out_specs=(VMEM,) * 4,
        scratch_shapes=[pltpu.VMEM((2, CT - 1, wide, 128), F32), pltpu.VMEM((8, 128), F32)],
        **params(10**7, 10**8),
    )(table, state, grade)
    strip = jax.ShapeDtypeStruct((7, CT, H, 128), F32)
    edge, to_up, to_down = pl.pallas_call(
        functools.partial(pack_x_kernel, ny),
        out_shape=(jax.ShapeDtypeStruct((7, rows, 128), F32), strip, strip),
        in_specs=[SMEM] + [VMEM] * 4 + [ANY],
        out_specs=(VMEM,) * 3,
        **params(2 * 10**6, 10**5),
    )(gy, state, grade, from_left, from_right, trace)
    top = lax.ppermute(to_down, "gx", ring(nx, 1))
    bottom = lax.ppermute(to_up, "gx", ring(nx, -1))
    keep, tail, trace, pe = pl.pallas_call(
        functools.partial(interior_kernel, ny),
        out_shape=(
            jax.ShapeDtypeStruct((6, CT, rows - H, 128), F32),
            jax.ShapeDtypeStruct((6, CT, H + 8, 128), F32),
            jax.ShapeDtypeStruct((4, CT, H, 128), F32),
            jax.ShapeDtypeStruct((8, wide, 128), F32),
        ),
        in_specs=[SMEM] + [VMEM] * 6,
        out_specs=(VMEM,) * 4,
        scratch_shapes=[
            pltpu.VMEM((6, CT, wide, 128), F32),
            pltpu.VMEM((2, CT, wide, 128), F32),
            pltpu.VMEM((8, 128), F32),
        ],
        **params(10**7, 10**8),
    )(gy, table, edge, st, pr, tail, trace)
    reach = 2 * H + 8
    return pl.pallas_call(
        functools.partial(exterior_kernel, ny),
        out_shape=jax.ShapeDtypeStruct((fields, rows, cols), F32),
        in_specs=[SMEM] + [VMEM] * 10,
        out_specs=VMEM,
        scratch_shapes=[pltpu.VMEM((planes, CT, reach, 128), F32) for planes in (6, 8, 6, 8)]
        + [pltpu.VMEM((8, 128), F32)],
        **params(10**7, 10**8),
    )(gy, table, grade, edge, keep, tail, trace, pr, pe, top, bottom)


def solution(mesh):
    placed = (P(None, "gx", "gy"), P("gx", "gy"), P())
    return jax.shard_map(
        shards, mesh=mesh, in_specs=placed, out_specs=P(None, "gx", "gy"), check_vma=False
    )
```

```python
import functools

import jax
import jax.numpy as jnp
from jax import lax
from jax.experimental import pallas as pl
from jax.experimental.pallas import tpu as pltpu
from jax.sharding import PartitionSpec as P

STEPS = 24
DT = 0.2
F32 = jnp.float32
H = 24
CT = 5
EDGE = 4
MAIN = (0, 1, 2, 3)
ALL = (0, 1, 2, 3, 4)
SWAP = 8
MID = 20
PACK = 4

VMEM = pl.BlockSpec(memory_space=pltpu.VMEM)
SMEM = pl.BlockSpec(memory_space=pltpu.SMEM)
ANY = pl.BlockSpec(memory_space=pl.ANY)


def lanes():
    return lax.broadcasted_iota(jnp.int32, (8, 128), 1)


def sublanes():
    return lax.broadcasted_iota(jnp.int32, (8, 128), 0)


def edge_live(gy, count):
    right = jnp.where(gy < count - 1, 1, 0)
    left = jnp.where(gy > 0, 1, 0)
    lane = lanes()
    return jnp.where(lane < H, left, jnp.where(lane >= 128 - H, right, 1)) > 0


def pack_y_kernel(state_hbm, grade_hbm, table_hbm, left_ref, right_ref, grade_ref, table_ref, ends, sems):
    rows, cols = state_hbm.shape[1:]
    group = rows // PACK
    lane = lanes()
    copies = []
    for f in range(6):
        for side, first in enumerate((0, cols - 128)):
            source = state_hbm.at[f, :, pl.ds(first, 128)]
            copies.append(pltpu.make_async_copy(source, ends.at[f, side], sems.at[2 * f + side]))
    copies.append(pltpu.make_async_copy(grade_hbm, grade_ref, sems.at[12]))
    copies.append(pltpu.make_async_copy(table_hbm, table_ref, sems.at[13]))
    for copy in copies:
        copy.start()

    def read(field, row, side):
        if field < 6:
            return ends[field, side, row : row + 8, :]
        first = side * (cols - 128)
        return grade_ref[row : row + 8, first : first + 128].astype(F32)

    for field in range(7):
        for copy in copies[2 * field : 2 * field + 2]:
            copy.wait()
        for k in range(group // 8):
            to_left = None
            to_right = None
            for q in range(PACK):
                row = q * group + 8 * k
                a = read(field, row, 0)
                b = read(field, row, 1)
                if q:
                    a = pltpu.roll(a, 32 * q, 1)
                b = pltpu.roll(b, 32 * q + H, 1)
                here = lane >= 32 * q
                to_left = a if q == 0 else jnp.where(here, a, to_left)
                to_right = b if q == 0 else jnp.where(here, b, to_right)
            left_ref[field, 8 * k : 8 * k + 8, :] = to_left
            right_ref[field, 8 * k : 8 * k + 8, :] = to_right


def pack_x_kernel(count, gy_ref, state_ref, grade_ref, from_left_ref, from_right_ref, _, edge_ref, up_ref, down_ref):
    rows, cols = state_ref.shape[1:]
    group = rows // PACK
    lane = lanes()
    live = edge_live(gy_ref[0], count)
    for field in range(7):
        for k in range(group // 8):
            right = from_right_ref[field, 8 * k : 8 * k + 8, :]
            left = from_left_ref[field, 8 * k : 8 * k + 8, :]
            for q in range(PACK):
                r = pltpu.roll(right, (128 - H - 32 * q) % 128, 1)
                s = left if q == 0 else pltpu.roll(left, 128 - 32 * q, 1)
                halo = jnp.where(lane < 64, s, r)
                if field < 6:
                    halo = jnp.where(live, halo, 0.0)
                row = q * group + 8 * k
                if field < 6:
                    first = state_ref[field, row : row + 8, 0:128]
                    last = state_ref[field, row : row + 8, cols - 128 : cols]
                else:
                    first = grade_ref[row : row + 8, 0:128].astype(F32)
                    last = grade_ref[row : row + 8, cols - 128 : cols].astype(F32)
                own = jnp.where(lane < 64, pltpu.roll(first, H, 1), pltpu.roll(last, 128 - H, 1))
                both = jnp.where((lane < H) | (lane >= 128 - H), halo, own)
                edge_ref[field, row : row + 8, :] = both
                if row < H:
                    up_ref[field, EDGE, row : row + 8, :] = both
                if row >= rows - H:
                    down_ref[field, EDGE, row - rows + H : row - rows + H + 8, :] = both
    for field in range(7):
        for c in MAIN:
            part = slice(128 * c, 128 * c + 128)
            if field < 6:
                up_ref[field, c] = state_ref[field, 0:H, part]
                down_ref[field, c] = state_ref[field, rows - H : rows, part]
            else:
                up_ref[field, c] = grade_ref[0:H, part].astype(F32)
                down_ref[field, c] = grade_ref[rows - H : rows, part].astype(F32)


def tables(table_ref, tab):
    tab[0:6, 0:16] = table_ref[...]

    def row(q):
        return jnp.broadcast_to(tab[q : q + 1, :], (8, 128))

    rate = row(4)
    return (
        0.25 * row(0),
        0.25 * row(1),
        0.25 * row(2),
        (DT * DT) * row(3),
        1.0 - rate,
        rate * row(5),
    )


def put_raw(pr, tabs, live, grade_of, cols, tiles, first_row, planes_=(0, 1, 3, 5, 6, 7)):
    for k in range(tiles):
        for c in cols:
            grade = grade_of(c, k)
            for t, q in enumerate((0, 1, 3, 5, 6, 7)):
                if q not in planes_:
                    continue
                value = jnp.take_along_axis(tabs[t], grade, axis=1)
                if c == EDGE and q in (5, 7):
                    value = jnp.where(live, value, 0.0)
                pr[q][c][pl.ds(first_row + 8 * k, 8), :] = value


def put_means(pr, live, cols, first_tile, tiles):
    for k in range(first_tile, first_tile + tiles):
        here = pl.ds(8 * k, 8)
        for q in (0, 1, 3):
            sums = {c: pr[q][c][here, :] + pr[q][c][pl.ds(8 * k + 1, 8), :] for c in cols}
            moved = following(sums)
            for c in cols:
                mean = sums[c] + moved[c]
                if c == EDGE:
                    mean = jnp.where(live, mean, 0.0)
                if q == 0:
                    pr[0][c][here, :] = mean
                elif q == 1:
                    pr[1][c][here, :] = 2.0 * mean
                    pr[2][c][here, :] = mean
                else:
                    pr[3][c][here, :] = mean
                    pr[4][c][here, :] = 0.125 * mean


def following(tiles):
    last = lanes() == 127
    rolled = {c: pltpu.roll(x, 127, 1) for c, x in tiles.items()}
    return {c: jnp.where(last, rolled[c + 1], rolled[c]) if c + 1 in MAIN and c in MAIN else rolled[c] for c in tiles}


def preceding(tiles):
    first = lanes() == 0
    rolled = {c: pltpu.roll(x, 1, 1) for c, x in tiles.items()}
    return {c: jnp.where(first, rolled[c - 1], rolled[c]) if c - 1 in MAIN and c in MAIN else rolled[c] for c in tiles}


def read(refs, rows):
    return {c: ref[rows, :] for c, ref in refs.items()}


def stresses(pr, rows, ux, uy, uxn, uyn):
    uxr = following(ux)
    uyr = following(uy)
    lam, mu2, mu, beta, beta8 = [read({c: pr[q][c] for c in ux}, rows) for q in range(5)]
    sxx, sxy, syy = {}, {}, {}
    for c in ux:
        exx = uxn[c] - ux[c]
        eyy = uyr[c] - uy[c]
        g = (uxr[c] - ux[c]) + (uyn[c] - uy[c])
        trace = lam[c] * (exx + eyy)
        sxx[c] = trace + exx * (mu2[c] + beta[c] * (exx * exx))
        syy[c] = trace + eyy * (mu2[c] + beta[c] * (eyy * eyy))
        sxy[c] = g * (mu[c] + beta8[c] * (g * g))
    sxy_l = preceding(sxy)
    syy_l = preceding(syy)
    gx = {c: sxx[c] + (sxy[c] - sxy_l[c]) for c in ux}
    gy = {c: sxy[c] + (syy[c] - syy_l[c]) for c in ux}
    return gx, gy, sxx, sxy


def update(st, pr, rows, ux, uy, gx, gy, px, py):
    dr, om, re = [read({c: pr[q][c] for c in ux}, rows) for q in (5, 6, 7)]
    vx, vy, wx, wy = [read({c: st[q][c] for c in ux}, rows) for q in (2, 3, 4, 5)]
    for c in ux:
        fx = gx[c] - px[c]
        fy = gy[c] - py[c]
        new_vx = vx[c] + dr[c] * (fx - wx[c])
        new_vy = vy[c] + dr[c] * (fy - wy[c])
        st[2][c][rows, :] = new_vx
        st[3][c][rows, :] = new_vy
        st[4][c][rows, :] = om[c] * wx[c] + re[c] * fx
        st[5][c][rows, :] = om[c] * wy[c] + re[c] * fy
        st[0][c][rows, :] = ux[c] + new_vx
        st[1][c][rows, :] = uy[c] + new_vy


def tiles_of(ref, cols):
    return [{c: ref.at[q, c] for c in cols} for q in range(ref.shape[0])]


def swap(st, first_row, rows):
    lane = lanes()
    inner = (lane >= H + MID) & (lane < 128 - H - MID)
    tiles = [pl.ds(8 * k, 8) for k in range(first_row // 8, (first_row + rows) // 8)]
    for f in range(6):
        old = [(st[f][EDGE][here, :], st[f][0][here, :], st[f][MAIN[-1]][here, :]) for here in tiles]
        new = []
        for edge, first, last in old:
            own = jnp.where(lane < 64, pltpu.roll(first, H, 1), pltpu.roll(last, 128 - H, 1))
            new.append((
                jnp.where(inner, own, edge),
                jnp.where(lane < MID, pltpu.roll(edge, 128 - H, 1), first),
                jnp.where(lane >= 128 - MID, pltpu.roll(edge, H, 1), last),
            ))
        for here, (edge, first, last) in zip(tiles, new):
            st[f][EDGE][here, :] = edge
            st[f][0][here, :] = first
            st[f][MAIN[-1]][here, :] = last


def trapezoid(st, pr, ss, cols, rows, groups, trace_ref, tail_ref):
    for g in groups:
        n = rows // 8 - g
        n = n + 1 if n == 8 else n

        def body(k, carry, n=n, g=g):
            base = 4 * g + k

            def at(offset):
                return pl.ds(base + offset, 8, stride=n)

            def u(f, offset):
                return read({c: st[f][c] for c in cols}, at(offset))

            ux, uy, uxn, uyn = u(0, 0), u(1, 0), u(0, 1), u(1, 1)
            gx0, gy0, px, py = stresses(pr, at(0), ux, uy, uxn, uyn)
            for c in cols:
                trace_ref[0, c, pl.ds(base, 1), :] = gx0[c][0:1]
                trace_ref[1, c, pl.ds(base, 1), :] = gy0[c][0:1]
            for r in range(n):
                ux, uy = uxn, uyn
                for c in cols:
                    ss[0, c, at(r), :] = px[c]
                    ss[1, c, at(r), :] = py[c]
                if r < n - 1:
                    uxn, uyn = u(0, r + 2), u(1, r + 2)
                    gx, gy, qx, qy = stresses(pr, at(r + 1), ux, uy, uxn, uyn)
                else:
                    gx = {c: pltpu.roll(v, 7, 0) for c, v in gx0.items()}
                    gy = {c: pltpu.roll(v, 7, 0) for c, v in gy0.items()}
                    qx, qy = px, py
                update(st, pr, at(r + 1), ux, uy, gx, gy, px, py)
                px, py = qx, qy
            row = pl.ds(rows - 2 - base, 1)
            for c in cols:
                for q in range(2):
                    trace_ref[2 + q, c, pl.ds(base, 1), :] = ss[q, c, row, :]
                for f in range(6):
                    tail_ref[f, c, pl.ds(H - 1 - base, 1), :] = st[f][c][row, :]
            return carry

        lax.fori_loop(0, 4, body, 0)


def own_kernel(table_ref, state_ref, grade_ref, st_ref, pr_ref, tail_ref, trace_ref, ss, tab):
    rows = state_ref.shape[1]
    tabs = tables(table_ref, tab)
    st, pr = tiles_of(st_ref, MAIN), tiles_of(pr_ref, MAIN)

    def grade_of(c, k):
        return grade_ref[8 * k : 8 * k + 8, 128 * c : 128 * c + 128]

    put_raw(pr, tabs, None, grade_of, MAIN, rows // 8, 0)
    put_means(pr, None, MAIN, 0, rows // 8)
    for f in range(6):
        for c in MAIN:
            block = state_ref[f, :, 128 * c : 128 * c + 128]
            if f in (2, 3):
                block = DT * block
            st[f][c][0:rows, :] = block
            tail_ref[f, c, H : H + 1, :] = block[rows - 1 : rows]
    trapezoid(st, pr, ss, MAIN, rows, range(SWAP // 4), trace_ref, tail_ref)


def interior_kernel(
    count, gy_ref, table_ref, edge_ref, st_ref, pr_ref, tail_in, trace_in, keep_ref, tail_ref, trace_ref, pe_ref, mid, ss, tab
):
    rows = edge_ref.shape[1]
    live = edge_live(gy_ref[0], count)
    tabs = tables(table_ref, tab)
    st = tiles_of(mid, ALL)
    pr = tiles_of(pr_ref, MAIN)
    for q in range(8):
        pr[q][EDGE] = pe_ref.at[q]

    def grade_of(c, k):
        return edge_ref[6, 8 * k : 8 * k + 8, :].astype(jnp.int32)

    put_raw(pr, tabs, live, grade_of, (EDGE,), rows // 8, 0)
    put_means(pr, live, (EDGE,), 0, rows // 8)
    for f in range(6):
        block = DT * edge_ref[f] if f in (2, 3) else edge_ref[f]
        st[f][EDGE][0:rows, :] = block
        tail_ref[f, EDGE, H : H + 1, :] = block[rows - 1 : rows]
        for c in MAIN:
            st[f][c][0:rows, :] = st_ref[f, c, 0:rows, :]
            tail_ref[f, c] = tail_in[f, c]
    for q in range(4):
        for c in MAIN:
            trace_ref[q, c] = trace_in[q, c]
    trapezoid(st, pr, ss, (EDGE,), rows, range(SWAP // 4), trace_ref, tail_ref)
    swap(st, 0, rows)
    trapezoid(st, pr, ss, ALL, rows, range(SWAP // 4, STEPS // 4), trace_ref, tail_ref)
    for f in range(6):
        for c in ALL:
            keep_ref[f, c] = st[f][c][0 : rows - H, :]


def exterior_kernel(
    count, gy_ref, table_ref, grade_ref, edge_ref, keep_ref, tail_ref, trace_ref, pr_ref, pe_ref, top_ref, bottom_ref,
    out_ref, sa_ref, pa_ref, sb_ref, pb_ref, hold, tab,
):
    rows = grade_ref.shape[0]
    live = edge_live(gy_ref[0], count)
    tabs = tables(table_ref, tab)
    near = H // 8
    sa, pa, sb, pb = [tiles_of(ref, ALL) for ref in (sa_ref, pa_ref, sb_ref, pb_ref)]

    def halo(ref):
        return lambda c, k: ref[6, c, 8 * k : 8 * k + 8, :].astype(jnp.int32)

    def own(row):
        def grade_of(c, k):
            if c == EDGE:
                return edge_ref[6, row : row + 8, :].astype(jnp.int32)
            return grade_ref[row : row + 8, 128 * c : 128 * c + 128]

        return grade_of

    def known(q, c, first, count_):
        return pe_ref[q, first : first + count_, :] if c == EDGE else pr_ref[q, c, first : first + count_, :]

    put_raw(pa, tabs, live, halo(top_ref), ALL, near, 0)
    put_raw(pa, tabs, live, own(0), ALL, 1, H, (0, 1, 3))
    put_means(pa, live, ALL, 0, near)
    put_raw(pb, tabs, live, own(rows - 8), ALL, 1, H - 8, (0, 1, 3))
    put_raw(pb, tabs, live, halo(bottom_ref), ALL, near, H)
    put_means(pb, live, ALL, near - 1, near + 1)
    for q in range(8):
        for c in ALL:
            pa[q][c][H : 2 * H, :] = known(q, c, 0, H)
            whole = H if q > 4 else H - 8
            pb[q][c][0:whole, :] = known(q, c, rows - H, whole)
    for f in range(6):
        for c in ALL:
            top = top_ref[f, c]
            bottom = bottom_ref[f, c]
            if f in (2, 3):
                top = DT * top
                bottom = DT * bottom
            sa[f][c][0:H, :] = top
            sa[f][c][H : 2 * H, :] = keep_ref[f, c, 0:H, :]
            sb[f][c][0:H, :] = tail_ref[f, c, 1 : H + 1, :]
            sb[f][c][H : 2 * H, :] = bottom

    sub = sublanes()
    n = near

    def trace(q, base):
        return [jnp.broadcast_to(trace_ref[q, c, pl.ds(base, 1), :], (8, 128)) for c in ALL]

    def b_rows(base, offset):
        return pl.ds(jnp.maximum(H - 1 - base, 0) + offset, 8, stride=n)

    def b_stress(base):
        ux = [read(sb[0], b_rows(base, r)) for r in range(n + 1)]
        uy = [read(sb[1], b_rows(base, r)) for r in range(n + 1)]
        for r in range(n):
            found = stresses(pb, b_rows(base, r), ux[r], uy[r], ux[r + 1], uy[r + 1])
            for q in range(4):
                for c in ALL:
                    hold[q, c, 8 * r : 8 * r + 8, :] = found[q][c]

    def b_update(base):
        def held(q, r):
            return {c: hold[q, c, 8 * r : 8 * r + 8, :] for c in ALL}

        for r in range(n):
            if r:
                px, py = held(2, r - 1), held(3, r - 1)
            else:
                tx, ty = trace(2, base), trace(3, base)
                lx, ly = held(2, n - 1), held(3, n - 1)
                px = {c: jnp.where(sub == 0, tx[c], pltpu.roll(lx[c], 1, 0)) for c in ALL}
                py = {c: jnp.where(sub == 0, ty[c], pltpu.roll(ly[c], 1, 0)) for c in ALL}
            rows_ = b_rows(base, r)
            update(sb, pb, rows_, read(sb[0], rows_), read(sb[1], rows_), held(0, r), held(1, r), px, py)

    def a_step(base):
        def at(offset):
            return pl.ds(base + offset, 8, stride=n)

        ux, uy = read(sa[0], at(0)), read(sa[1], at(0))
        uxn, uyn = read(sa[0], at(1)), read(sa[1], at(1))
        gx0, gy0, px, py = stresses(pa, at(0), ux, uy, uxn, uyn)
        for r in range(n):
            ux, uy = uxn, uyn
            if r < n - 1:
                uxn, uyn = read(sa[0], at(r + 2)), read(sa[1], at(r + 2))
                gx, gy, qx, qy = stresses(pa, at(r + 1), ux, uy, uxn, uyn)
            else:
                tx, ty = trace(0, base), trace(1, base)
                gx = {c: jnp.where(sub == 7, tx[c], pltpu.roll(gx0[c], 7, 0)) for c in ALL}
                gy = {c: jnp.where(sub == 7, ty[c], pltpu.roll(gy0[c], 7, 0)) for c in ALL}
                qx, qy = px, py
            update(sa, pa, at(r + 1), ux, uy, gx, gy, px, py)
            px, py = qx, qy

    def body(base, carry):
        b_update(base)
        a_step(base)
        b_stress(base + 1)
        return carry

    b_stress(0)
    lax.fori_loop(0, SWAP, body, 0)
    swap(sa, SWAP, H)
    swap(sb, H - 2 * SWAP, H + SWAP)
    b_stress(SWAP)
    lax.fori_loop(SWAP, STEPS, body, 0)
    lane = lanes()
    for f in range(6):
        for k in range(rows // 8):
            row = 8 * k

            def final(c):
                if row < H:
                    return sa[f][c][H + row : H + row + 8, :]
                if row < rows - H:
                    return keep_ref[f, c, row : row + 8, :]
                return sb[f][c][row - rows + H : row - rows + H + 8, :]

            edge = final(EDGE)
            for c in MAIN:
                value = final(c)
                if c == 0:
                    value = jnp.where(lane < MID, pltpu.roll(edge, 128 - H, 1), value)
                if c == MAIN[-1]:
                    value = jnp.where(lane >= 128 - MID, pltpu.roll(edge, H, 1), value)
                if f in (2, 3):
                    value = (1.0 / DT) * value
                out_ref[f, row : row + 8, 128 * c : 128 * c + 128] = value


def params(bytes_, flops, mib=24):
    return dict(
        compiler_params=pltpu.CompilerParams(vmem_limit_bytes=int(mib * 2**20)),
        cost_estimate=pl.CostEstimate(flops=flops, bytes_accessed=bytes_, transcendentals=0),
    )


def ring(count, step):
    return [(i, (i + step) % count) for i in range(count)]


def shards(state, grade, table):
    fields, rows, cols = state.shape
    nx = lax.axis_size("gx")
    ny = lax.axis_size("gy")
    gy = jnp.full((1,), lax.axis_index("gy"), jnp.int32)
    packed = jax.ShapeDtypeStruct((7, rows // PACK, 128), F32)
    to_left, to_right, grade, table = pl.pallas_call(
        pack_y_kernel,
        out_shape=(
            packed,
            packed,
            jax.ShapeDtypeStruct(grade.shape, grade.dtype),
            jax.ShapeDtypeStruct(table.shape, table.dtype),
        ),
        in_specs=[ANY] * 3,
        out_specs=(VMEM,) * 4,
        scratch_shapes=[pltpu.VMEM((6, 2, rows, 128), F32), pltpu.SemaphoreType.DMA((14,))],
        **params(10**6, 10**5, 53.6),
    )(state, grade, table)
    from_left = lax.ppermute(to_right, "gy", ring(ny, 1))
    from_right = lax.ppermute(to_left, "gy", ring(ny, -1))
    wide = rows + 16
    st, pr, tail, trace = pl.pallas_call(
        own_kernel,
        out_shape=(
            jax.ShapeDtypeStruct((6, CT - 1, wide, 128), F32),
            jax.ShapeDtypeStruct((8, CT - 1, wide, 128), F32),
            jax.ShapeDtypeStruct((6, CT - 1, H + 8, 128), F32),
            jax.ShapeDtypeStruct((4, CT - 1, H, 128), F32),
        ),
        in_specs=[VMEM] * 3,
        out_specs=(VMEM,) * 4,
        scratch_shapes=[pltpu.VMEM((2, CT - 1, wide, 128), F32), pltpu.VMEM((8, 128), F32)],
        **params(10**7, 10**8),
    )(table, state, grade)
    strip = jax.ShapeDtypeStruct((7, CT, H, 128), F32)
    edge, to_up, to_down = pl.pallas_call(
        functools.partial(pack_x_kernel, ny),
        out_shape=(jax.ShapeDtypeStruct((7, rows, 128), F32), strip, strip),
        in_specs=[SMEM] + [VMEM] * 4 + [ANY],
        out_specs=(VMEM,) * 3,
        **params(2 * 10**6, 10**5),
    )(gy, state, grade, from_left, from_right, trace)
    top = lax.ppermute(to_down, "gx", ring(nx, 1))
    bottom = lax.ppermute(to_up, "gx", ring(nx, -1))
    keep, tail, trace, pe = pl.pallas_call(
        functools.partial(interior_kernel, ny),
        out_shape=(
            jax.ShapeDtypeStruct((6, CT, rows - H, 128), F32),
            jax.ShapeDtypeStruct((6, CT, H + 8, 128), F32),
            jax.ShapeDtypeStruct((4, CT, H, 128), F32),
            jax.ShapeDtypeStruct((8, wide, 128), F32),
        ),
        in_specs=[SMEM] + [VMEM] * 6,
        out_specs=(VMEM,) * 4,
        scratch_shapes=[
            pltpu.VMEM((6, CT, wide, 128), F32),
            pltpu.VMEM((2, CT, wide, 128), F32),
            pltpu.VMEM((8, 128), F32),
        ],
        **params(10**7, 10**8),
    )(gy, table, edge, st, pr, tail, trace)
    reach = 2 * H + 8
    return pl.pallas_call(
        functools.partial(exterior_kernel, ny),
        out_shape=jax.ShapeDtypeStruct((fields, rows, cols), F32),
        in_specs=[SMEM] + [VMEM] * 10,
        out_specs=VMEM,
        scratch_shapes=[pltpu.VMEM((planes, CT, reach, 128), F32) for planes in (6, 8, 6, 8)]
        + [pltpu.VMEM((4, CT, H, 128), F32), pltpu.VMEM((8, 128), F32)],
        **params(10**7, 10**8),
    )(gy, table, grade, edge, keep, tail, trace, pr, pe, top, bottom)


def solution(mesh):
    placed = (P(None, "gx", "gy"), P("gx", "gy"), P())
    return jax.shard_map(
        shards, mesh=mesh, in_specs=placed, out_specs=P(None, "gx", "gy"), check_vma=False
    )
```

```python
import functools

import jax
import jax.numpy as jnp
from jax import lax
from jax.experimental import pallas as pl
from jax.experimental.pallas import tpu as pltpu
from jax.sharding import PartitionSpec as P

STEPS = 24
DT = 0.2
F32 = jnp.float32
H = 24
CT = 5
EDGE = 4
MAIN = (0, 1, 2, 3)
ALL = (0, 1, 2, 3, 4)
SWAP = 8
MID = 20
PACK = 4

VMEM = pl.BlockSpec(memory_space=pltpu.VMEM)
SMEM = pl.BlockSpec(memory_space=pltpu.SMEM)
ANY = pl.BlockSpec(memory_space=pl.ANY)


def lanes():
    return lax.broadcasted_iota(jnp.int32, (8, 128), 1)


def sublanes():
    return lax.broadcasted_iota(jnp.int32, (8, 128), 0)


def edge_live(gy, count):
    right = jnp.where(gy < count - 1, 1, 0)
    left = jnp.where(gy > 0, 1, 0)
    lane = lanes()
    return jnp.where(lane < H, left, jnp.where(lane >= 128 - H, right, 1)) > 0


def pack_y_kernel(state_hbm, grade_hbm, table_hbm, left_ref, right_ref, grade_ref, table_ref, ends, sems):
    rows, cols = state_hbm.shape[1:]
    group = rows // PACK
    lane = lanes()
    copies = []
    for f in range(6):
        for side, first in enumerate((0, cols - 128)):
            source = state_hbm.at[f, :, pl.ds(first, 128)]
            copies.append(pltpu.make_async_copy(source, ends.at[f, side], sems.at[2 * f + side]))
    copies.append(pltpu.make_async_copy(grade_hbm, grade_ref, sems.at[12]))
    copies.append(pltpu.make_async_copy(table_hbm, table_ref, sems.at[13]))
    for copy in copies:
        copy.start()

    def read(field, row, side):
        if field < 6:
            return ends[field, side, row : row + 8, :]
        first = side * (cols - 128)
        return grade_ref[row : row + 8, first : first + 128].astype(F32)

    for field in range(7):
        for copy in copies[2 * field : 2 * field + 2]:
            copy.wait()
        for k in range(group // 8):
            to_left = None
            to_right = None
            for q in range(PACK):
                row = q * group + 8 * k
                a = read(field, row, 0)
                b = read(field, row, 1)
                if q:
                    a = pltpu.roll(a, 32 * q, 1)
                b = pltpu.roll(b, 32 * q + H, 1)
                here = lane >= 32 * q
                to_left = a if q == 0 else jnp.where(here, a, to_left)
                to_right = b if q == 0 else jnp.where(here, b, to_right)
            left_ref[field, 8 * k : 8 * k + 8, :] = to_left
            right_ref[field, 8 * k : 8 * k + 8, :] = to_right


def pack_x_kernel(count, gy_ref, state_ref, grade_ref, from_left_ref, from_right_ref, _, edge_ref, up_ref, down_ref):
    rows, cols = state_ref.shape[1:]
    group = rows // PACK
    lane = lanes()
    live = edge_live(gy_ref[0], count)
    for field in range(7):
        for k in range(group // 8):
            right = from_right_ref[field, 8 * k : 8 * k + 8, :]
            left = from_left_ref[field, 8 * k : 8 * k + 8, :]
            for q in range(PACK):
                r = pltpu.roll(right, (128 - H - 32 * q) % 128, 1)
                s = left if q == 0 else pltpu.roll(left, 128 - 32 * q, 1)
                halo = jnp.where(lane < 64, s, r)
                if field < 6:
                    halo = jnp.where(live, halo, 0.0)
                row = q * group + 8 * k
                if field < 6:
                    first = state_ref[field, row : row + 8, 0:128]
                    last = state_ref[field, row : row + 8, cols - 128 : cols]
                else:
                    first = grade_ref[row : row + 8, 0:128].astype(F32)
                    last = grade_ref[row : row + 8, cols - 128 : cols].astype(F32)
                own = jnp.where(lane < 64, pltpu.roll(first, H, 1), pltpu.roll(last, 128 - H, 1))
                both = jnp.where((lane < H) | (lane >= 128 - H), halo, own)
                edge_ref[field, row : row + 8, :] = both
                if row < H:
                    up_ref[field, EDGE, row : row + 8, :] = both
                if row >= rows - H:
                    down_ref[field, EDGE, row - rows + H : row - rows + H + 8, :] = both
    for field in range(7):
        for c in MAIN:
            part = slice(128 * c, 128 * c + 128)
            if field < 6:
                up_ref[field, c] = state_ref[field, 0:H, part]
                down_ref[field, c] = state_ref[field, rows - H : rows, part]
            else:
                up_ref[field, c] = grade_ref[0:H, part].astype(F32)
                down_ref[field, c] = grade_ref[rows - H : rows, part].astype(F32)


def tables(table_ref, tab):
    tab[0:6, 0:16] = table_ref[...]

    def row(q):
        return jnp.broadcast_to(tab[q : q + 1, :], (8, 128))

    rate = row(4)
    return (
        0.25 * row(0),
        0.25 * row(1),
        0.25 * row(2),
        (DT * DT) * row(3),
        1.0 - rate,
        rate * row(5),
    )


def put_raw(pr, tabs, live, grade_of, cols, tiles, first_row, planes_=(0, 1, 3, 5, 6, 7)):
    for k in range(tiles):
        for c in cols:
            grade = grade_of(c, k)
            for t, q in enumerate((0, 1, 3, 5, 6, 7)):
                if q not in planes_:
                    continue
                value = jnp.take_along_axis(tabs[t], grade, axis=1)
                if c == EDGE and q in (5, 7):
                    value = jnp.where(live, value, 0.0)
                pr[q][c][pl.ds(first_row + 8 * k, 8), :] = value


def put_means(pr, live, cols, first_tile, tiles):
    for k in range(first_tile, first_tile + tiles):
        here = pl.ds(8 * k, 8)
        for q in (0, 1, 3):
            sums = {c: pr[q][c][here, :] + pr[q][c][pl.ds(8 * k + 1, 8), :] for c in cols}
            moved = following(sums)
            for c in cols:
                mean = sums[c] + moved[c]
                if c == EDGE:
                    mean = jnp.where(live, mean, 0.0)
                if q == 0:
                    pr[0][c][here, :] = mean
                elif q == 1:
                    pr[1][c][here, :] = 2.0 * mean
                    pr[2][c][here, :] = mean
                else:
                    pr[3][c][here, :] = mean
                    pr[4][c][here, :] = 0.125 * mean


def following(tiles):
    last = lanes() == 127
    rolled = {c: pltpu.roll(x, 127, 1) for c, x in tiles.items()}
    return {c: jnp.where(last, rolled[c + 1], rolled[c]) if c + 1 in MAIN and c in MAIN else rolled[c] for c in tiles}


def preceding(tiles):
    first = lanes() == 0
    rolled = {c: pltpu.roll(x, 1, 1) for c, x in tiles.items()}
    return {c: jnp.where(first, rolled[c - 1], rolled[c]) if c - 1 in MAIN and c in MAIN else rolled[c] for c in tiles}


def read(refs, rows):
    return {c: ref[rows, :] for c, ref in refs.items()}


def stresses(pr, rows, ux, uy, uxn, uyn):
    uxr = following(ux)
    uyr = following(uy)
    lam, mu2, mu, beta, beta8 = [read({c: pr[q][c] for c in ux}, rows) for q in range(5)]
    sxx, sxy, syy = {}, {}, {}
    for c in ux:
        exx = uxn[c] - ux[c]
        eyy = uyr[c] - uy[c]
        g = (uxr[c] - ux[c]) + (uyn[c] - uy[c])
        trace = lam[c] * (exx + eyy)
        sxx[c] = trace + exx * (mu2[c] + beta[c] * (exx * exx))
        syy[c] = trace + eyy * (mu2[c] + beta[c] * (eyy * eyy))
        sxy[c] = g * (mu[c] + beta8[c] * (g * g))
    sxy_l = preceding(sxy)
    syy_l = preceding(syy)
    gx = {c: sxx[c] + (sxy[c] - sxy_l[c]) for c in ux}
    gy = {c: sxy[c] + (syy[c] - syy_l[c]) for c in ux}
    return gx, gy, sxx, sxy


def update(st, pr, rows, ux, uy, gx, gy, px, py):
    dr, om, re = [read({c: pr[q][c] for c in ux}, rows) for q in (5, 6, 7)]
    vx, vy, wx, wy = [read({c: st[q][c] for c in ux}, rows) for q in (2, 3, 4, 5)]
    for c in ux:
        fx = gx[c] - px[c]
        fy = gy[c] - py[c]
        new_vx = vx[c] + dr[c] * (fx - wx[c])
        new_vy = vy[c] + dr[c] * (fy - wy[c])
        st[2][c][rows, :] = new_vx
        st[3][c][rows, :] = new_vy
        st[4][c][rows, :] = om[c] * wx[c] + re[c] * fx
        st[5][c][rows, :] = om[c] * wy[c] + re[c] * fy
        st[0][c][rows, :] = ux[c] + new_vx
        st[1][c][rows, :] = uy[c] + new_vy


def tiles_of(ref, cols):
    return [{c: ref.at[q, c] for c in cols} for q in range(ref.shape[0])]


def swap(st, first_row, rows):
    lane = lanes()
    inner = (lane >= H + MID) & (lane < 128 - H - MID)
    tiles = [pl.ds(8 * k, 8) for k in range(first_row // 8, (first_row + rows) // 8)]
    for f in range(6):
        old = [(st[f][EDGE][here, :], st[f][0][here, :], st[f][MAIN[-1]][here, :]) for here in tiles]
        new = []
        for edge, first, last in old:
            own = jnp.where(lane < 64, pltpu.roll(first, H, 1), pltpu.roll(last, 128 - H, 1))
            new.append((
                jnp.where(inner, own, edge),
                jnp.where(lane < MID, pltpu.roll(edge, 128 - H, 1), first),
                jnp.where(lane >= 128 - MID, pltpu.roll(edge, H, 1), last),
            ))
        for here, (edge, first, last) in zip(tiles, new):
            st[f][EDGE][here, :] = edge
            st[f][0][here, :] = first
            st[f][MAIN[-1]][here, :] = last


def trapezoid(st, pr, ss, cols, rows, groups, trace_ref, tail_ref):
    for g in groups:
        n = rows // 8 - g
        n = n + 1 if n == 8 else n

        def body(k, carry, n=n, g=g):
            base = 4 * g + k

            def at(offset):
                return pl.ds(base + offset, 8, stride=n)

            def u(f, offset):
                return read({c: st[f][c] for c in cols}, at(offset))

            ux, uy, uxn, uyn = u(0, 0), u(1, 0), u(0, 1), u(1, 1)
            gx0, gy0, px, py = stresses(pr, at(0), ux, uy, uxn, uyn)
            for c in cols:
                trace_ref[0, c, pl.ds(base, 1), :] = gx0[c][0:1]
                trace_ref[1, c, pl.ds(base, 1), :] = gy0[c][0:1]
            for r in range(n):
                ux, uy = uxn, uyn
                for c in cols:
                    ss[0, c, at(r), :] = px[c]
                    ss[1, c, at(r), :] = py[c]
                if r < n - 1:
                    uxn, uyn = u(0, r + 2), u(1, r + 2)
                    gx, gy, qx, qy = stresses(pr, at(r + 1), ux, uy, uxn, uyn)
                else:
                    gx = {c: pltpu.roll(v, 7, 0) for c, v in gx0.items()}
                    gy = {c: pltpu.roll(v, 7, 0) for c, v in gy0.items()}
                    qx, qy = px, py
                update(st, pr, at(r + 1), ux, uy, gx, gy, px, py)
                px, py = qx, qy
            row = pl.ds(rows - 2 - base, 1)
            for c in cols:
                for q in range(2):
                    trace_ref[2 + q, c, pl.ds(base, 1), :] = ss[q, c, row, :]
                for f in range(6):
                    tail_ref[f, c, pl.ds(H - 1 - base, 1), :] = st[f][c][row, :]
            return carry

        lax.fori_loop(0, 4, body, 0)


def own_kernel(table_ref, state_ref, grade_ref, st_ref, pr_ref, tail_ref, trace_ref, ss, tab):
    rows = state_ref.shape[1]
    tabs = tables(table_ref, tab)
    st, pr = tiles_of(st_ref, MAIN), tiles_of(pr_ref, MAIN)

    def grade_of(c, k):
        return grade_ref[8 * k : 8 * k + 8, 128 * c : 128 * c + 128]

    put_raw(pr, tabs, None, grade_of, MAIN, rows // 8, 0)
    put_means(pr, None, MAIN, 0, rows // 8)
    for f in range(6):
        for c in MAIN:
            block = state_ref[f, :, 128 * c : 128 * c + 128]
            if f in (2, 3):
                block = DT * block
            st[f][c][0:rows, :] = block
            tail_ref[f, c, H : H + 1, :] = block[rows - 1 : rows]
    trapezoid(st, pr, ss, MAIN, rows, range(SWAP // 4), trace_ref, tail_ref)


def interior_kernel(
    count, gy_ref, table_ref, edge_ref, st_ref, pr_ref, tail_in, trace_in, keep_ref, tail_ref, trace_ref, pe_ref, mid, ss, tab
):
    rows = edge_ref.shape[1]
    live = edge_live(gy_ref[0], count)
    tabs = tables(table_ref, tab)
    st = tiles_of(mid, ALL)
    pr = tiles_of(pr_ref, MAIN)
    for q in range(8):
        pr[q][EDGE] = pe_ref.at[q]

    def grade_of(c, k):
        return edge_ref[6, 8 * k : 8 * k + 8, :].astype(jnp.int32)

    put_raw(pr, tabs, live, grade_of, (EDGE,), rows // 8, 0)
    put_means(pr, live, (EDGE,), 0, rows // 8)
    for f in range(6):
        block = DT * edge_ref[f] if f in (2, 3) else edge_ref[f]
        st[f][EDGE][0:rows, :] = block
        tail_ref[f, EDGE, H : H + 1, :] = block[rows - 1 : rows]
        for c in MAIN:
            st[f][c][0:rows, :] = st_ref[f, c, 0:rows, :]
            tail_ref[f, c] = tail_in[f, c]
    for q in range(4):
        for c in MAIN:
            trace_ref[q, c] = trace_in[q, c]
    trapezoid(st, pr, ss, (EDGE,), rows, range(SWAP // 4), trace_ref, tail_ref)
    swap(st, SWAP, rows - 2 * SWAP)
    trapezoid(st, pr, ss, ALL, rows, range(SWAP // 4, STEPS // 4), trace_ref, tail_ref)
    for f in range(6):
        for c in ALL:
            keep_ref[f, c] = st[f][c][0 : rows - H, :]


def exterior_kernel(
    count, gy_ref, table_ref, grade_ref, edge_ref, keep_ref, tail_ref, trace_ref, pr_ref, pe_ref, top_ref, bottom_ref,
    out_ref, sa_ref, pa_ref, sb_ref, pb_ref, hold, tab,
):
    rows = grade_ref.shape[0]
    live = edge_live(gy_ref[0], count)
    tabs = tables(table_ref, tab)
    near = H // 8
    sa, pa, sb, pb = [tiles_of(ref, ALL) for ref in (sa_ref, pa_ref, sb_ref, pb_ref)]

    def halo(ref):
        return lambda c, k: ref[6, c, 8 * k : 8 * k + 8, :].astype(jnp.int32)

    def own(row):
        def grade_of(c, k):
            if c == EDGE:
                return edge_ref[6, row : row + 8, :].astype(jnp.int32)
            return grade_ref[row : row + 8, 128 * c : 128 * c + 128]

        return grade_of

    def known(q, c, first, count_):
        return pe_ref[q, first : first + count_, :] if c == EDGE else pr_ref[q, c, first : first + count_, :]

    put_raw(pa, tabs, live, halo(top_ref), ALL, near, 0)
    put_raw(pa, tabs, live, own(0), ALL, 1, H, (0, 1, 3))
    put_means(pa, live, ALL, 0, near)
    put_raw(pb, tabs, live, own(rows - 8), ALL, 1, H - 8, (0, 1, 3))
    put_raw(pb, tabs, live, halo(bottom_ref), ALL, near, H)
    put_means(pb, live, ALL, near - 1, near + 1)
    for q in range(8):
        for c in ALL:
            pa[q][c][H : 2 * H, :] = known(q, c, 0, H)
            whole = H if q > 4 else H - 8
            pb[q][c][0:whole, :] = known(q, c, rows - H, whole)
    for f in range(6):
        for c in ALL:
            top = top_ref[f, c]
            bottom = bottom_ref[f, c]
            if f in (2, 3):
                top = DT * top
                bottom = DT * bottom
            sa[f][c][0:H, :] = top
            sa[f][c][H : 2 * H, :] = keep_ref[f, c, 0:H, :]
            sb[f][c][0:H, :] = tail_ref[f, c, 1 : H + 1, :]
            sb[f][c][H : 2 * H, :] = bottom

    sub = sublanes()
    n = near

    def trace(q, base):
        return [jnp.broadcast_to(trace_ref[q, c, pl.ds(base, 1), :], (8, 128)) for c in ALL]

    def b_rows(base, offset):
        return pl.ds(jnp.maximum(H - 1 - base, 0) + offset, 8, stride=n)

    def b_stress(base):
        ux = [read(sb[0], b_rows(base, r)) for r in range(n + 1)]
        uy = [read(sb[1], b_rows(base, r)) for r in range(n + 1)]
        for r in range(n):
            found = stresses(pb, b_rows(base, r), ux[r], uy[r], ux[r + 1], uy[r + 1])
            for q in range(4):
                for c in ALL:
                    hold[q, c, 8 * r : 8 * r + 8, :] = found[q][c]

    def b_update(base):
        def held(q, r):
            return {c: hold[q, c, 8 * r : 8 * r + 8, :] for c in ALL}

        for r in range(n):
            if r:
                px, py = held(2, r - 1), held(3, r - 1)
            else:
                tx, ty = trace(2, base), trace(3, base)
                lx, ly = held(2, n - 1), held(3, n - 1)
                px = {c: jnp.where(sub == 0, tx[c], pltpu.roll(lx[c], 1, 0)) for c in ALL}
                py = {c: jnp.where(sub == 0, ty[c], pltpu.roll(ly[c], 1, 0)) for c in ALL}
            rows_ = b_rows(base, r)
            update(sb, pb, rows_, read(sb[0], rows_), read(sb[1], rows_), held(0, r), held(1, r), px, py)

    def a_step(base):
        def at(offset):
            return pl.ds(base + offset, 8, stride=n)

        ux, uy = read(sa[0], at(0)), read(sa[1], at(0))
        uxn, uyn = read(sa[0], at(1)), read(sa[1], at(1))
        gx0, gy0, px, py = stresses(pa, at(0), ux, uy, uxn, uyn)
        for r in range(n):
            ux, uy = uxn, uyn
            if r < n - 1:
                uxn, uyn = read(sa[0], at(r + 2)), read(sa[1], at(r + 2))
                gx, gy, qx, qy = stresses(pa, at(r + 1), ux, uy, uxn, uyn)
            else:
                tx, ty = trace(0, base), trace(1, base)
                gx = {c: jnp.where(sub == 7, tx[c], pltpu.roll(gx0[c], 7, 0)) for c in ALL}
                gy = {c: jnp.where(sub == 7, ty[c], pltpu.roll(gy0[c], 7, 0)) for c in ALL}
                qx, qy = px, py
            update(sa, pa, at(r + 1), ux, uy, gx, gy, px, py)
            px, py = qx, qy

    def body(base, carry):
        b_update(base)
        a_step(base)
        b_stress(base + 1)
        return carry

    b_stress(0)
    lax.fori_loop(0, SWAP, body, 0)
    swap(sa, SWAP, H)
    swap(sb, H - 2 * SWAP, H + SWAP)
    b_stress(SWAP)
    lax.fori_loop(SWAP, STEPS, body, 0)
    lane = lanes()
    for f in range(6):
        for k in range(rows // 8):
            row = 8 * k

            def final(c):
                if row < H:
                    return sa[f][c][H + row : H + row + 8, :]
                if row < rows - H:
                    return keep_ref[f, c, row : row + 8, :]
                return sb[f][c][row - rows + H : row - rows + H + 8, :]

            edge = final(EDGE)
            for c in MAIN:
                value = final(c)
                if c == 0:
                    value = jnp.where(lane < MID, pltpu.roll(edge, 128 - H, 1), value)
                if c == MAIN[-1]:
                    value = jnp.where(lane >= 128 - MID, pltpu.roll(edge, H, 1), value)
                if f in (2, 3):
                    value = (1.0 / DT) * value
                out_ref[f, row : row + 8, 128 * c : 128 * c + 128] = value


def params(bytes_, flops, mib=24):
    return dict(
        compiler_params=pltpu.CompilerParams(vmem_limit_bytes=int(mib * 2**20)),
        cost_estimate=pl.CostEstimate(flops=flops, bytes_accessed=bytes_, transcendentals=0),
    )


def ring(count, step):
    return [(i, (i + step) % count) for i in range(count)]


def shards(state, grade, table):
    fields, rows, cols = state.shape
    nx = lax.axis_size("gx")
    ny = lax.axis_size("gy")
    gy = jnp.full((1,), lax.axis_index("gy"), jnp.int32)
    packed = jax.ShapeDtypeStruct((7, rows // PACK, 128), F32)
    to_left, to_right, grade, table = pl.pallas_call(
        pack_y_kernel,
        out_shape=(
            packed,
            packed,
            jax.ShapeDtypeStruct(grade.shape, grade.dtype),
            jax.ShapeDtypeStruct(table.shape, table.dtype),
        ),
        in_specs=[ANY] * 3,
        out_specs=(VMEM,) * 4,
        scratch_shapes=[pltpu.VMEM((6, 2, rows, 128), F32), pltpu.SemaphoreType.DMA((14,))],
        **params(10**6, 10**5, 53.6),
    )(state, grade, table)
    from_left = lax.ppermute(to_right, "gy", ring(ny, 1))
    from_right = lax.ppermute(to_left, "gy", ring(ny, -1))
    wide = rows + 16
    st, pr, tail, trace = pl.pallas_call(
        own_kernel,
        out_shape=(
            jax.ShapeDtypeStruct((6, CT - 1, wide, 128), F32),
            jax.ShapeDtypeStruct((8, CT - 1, wide, 128), F32),
            jax.ShapeDtypeStruct((6, CT - 1, H + 8, 128), F32),
            jax.ShapeDtypeStruct((4, CT - 1, H, 128), F32),
        ),
        in_specs=[VMEM] * 3,
        out_specs=(VMEM,) * 4,
        scratch_shapes=[pltpu.VMEM((2, CT - 1, wide, 128), F32), pltpu.VMEM((8, 128), F32)],
        **params(10**7, 10**8),
    )(table, state, grade)
    strip = jax.ShapeDtypeStruct((7, CT, H, 128), F32)
    edge, to_up, to_down = pl.pallas_call(
        functools.partial(pack_x_kernel, ny),
        out_shape=(jax.ShapeDtypeStruct((7, rows, 128), F32), strip, strip),
        in_specs=[SMEM] + [VMEM] * 4 + [ANY],
        out_specs=(VMEM,) * 3,
        **params(2 * 10**6, 10**5),
    )(gy, state, grade, from_left, from_right, trace)
    top = lax.ppermute(to_down, "gx", ring(nx, 1))
    bottom = lax.ppermute(to_up, "gx", ring(nx, -1))
    keep, tail, trace, pe = pl.pallas_call(
        functools.partial(interior_kernel, ny),
        out_shape=(
            jax.ShapeDtypeStruct((6, CT, rows - H, 128), F32),
            jax.ShapeDtypeStruct((6, CT, H + 8, 128), F32),
            jax.ShapeDtypeStruct((4, CT, H, 128), F32),
            jax.ShapeDtypeStruct((8, wide, 128), F32),
        ),
        in_specs=[SMEM] + [VMEM] * 6,
        out_specs=(VMEM,) * 4,
        scratch_shapes=[
            pltpu.VMEM((6, CT, wide, 128), F32),
            pltpu.VMEM((2, CT, wide, 128), F32),
            pltpu.VMEM((8, 128), F32),
        ],
        **params(10**7, 10**8),
    )(gy, table, edge, st, pr, tail, trace)
    reach = 2 * H + 8
    return pl.pallas_call(
        functools.partial(exterior_kernel, ny),
        out_shape=jax.ShapeDtypeStruct((fields, rows, cols), F32),
        in_specs=[SMEM] + [VMEM] * 10,
        out_specs=VMEM,
        scratch_shapes=[pltpu.VMEM((planes, CT, reach, 128), F32) for planes in (6, 8, 6, 8)]
        + [pltpu.VMEM((4, CT, H, 128), F32), pltpu.VMEM((8, 128), F32)],
        **params(10**7, 10**8),
    )(gy, table, grade, edge, keep, tail, trace, pr, pe, top, bottom)


def solution(mesh):
    placed = (P(None, "gx", "gy"), P("gx", "gy"), P())
    return jax.shard_map(
        shards, mesh=mesh, in_specs=placed, out_specs=P(None, "gx", "gy"), check_vma=False
    )
```
